512 devices in a mesh: ia: 8 (over y_hi, x), ja: 16 (over z, core), ka: 4 (over y_lo).
Axes of the slice: x: 4, y: 8 (y_hi: 2, y_lo: 4; y = y_hi * 4 + y_lo), z: 8, core: 2. Of those that a mesh axis runs over, the one named last changes fastest.
Arguments:
- slab: float32 [256, 1024, 1024], P('ia', 'ja', 'ka'), may hold values from -8 to 8
- factor_two: float32 [1024, 48], P('ja'), may hold values from -0.1875 to 0.1875
- factor_three: float32 [1024, 48], P('ka'), may hold values from -0.1875 to 0.1875
Outputs:
- core: float32 [256, 2304], P('ia', ('ja', 'ka'))
- gram: float32 [256, 256], P('ia')
The draws below stay inside these ranges and needn't reach their ends.
All inputs are finite; a program needn't handle non-finite values.
Results may differ from the reference program's by a relative error of at most 0.00007.
Values sent between devices are 32-bit elements; how exact they have to be, the bound alone decides.
No kernel may reach another device: no remote copies, remote signals or barrier semaphores. Data moves between devices by JAX's collectives and lax.ppermute only.
A program may use at most 64 MiB of HBM per device.

```python
import jax
import jax.numpy as jnp
from jax import lax

R = 48
CI = 32
I = 256
J = 1024
K = 1024
N_IA = 8


def shard_levels(own_key, shape, pieces, smallest, high):
    def one(axis_at, parts):
        draws = jax.random.uniform(jax.random.fold_in(jax.random.fold_in(own_key, 6), axis_at), (parts,), jnp.float32, smallest / len(pieces), high / len(pieces))
        return jnp.repeat(jnp.exp(draws), shape[axis_at] // parts).reshape((-1,) + (1,) * (len(shape) - axis_at - 1))

    gain = one(*pieces[0])
    for cut in pieces[1:]:
        gain = gain * one(*cut)
    return gain


def noise(key, dims, width, bound, pieces=(), dtype=jnp.bfloat16):
    array = jax.random.normal(key, dims, jnp.float32) * width
    if len(pieces) > 0:
        array = shard_levels(key, dims, pieces, -0.22, 0.18) * array
    return jnp.clip(array, min=-bound, max=bound).astype(dtype)


def setup_inputs(seed: int = 0) -> dict:
    seeds = jax.random.split(jax.random.key(seed), 4)
    return {
        "slab": noise(seeds[0], (I, J, K), 1.0, 8.0, ((0, 8), (1, 16), (2, 4)), jnp.float32),
        "factor_two": noise(seeds[1], (J, R), J ** -0.5, 0.1875, ((0, 16),), jnp.float32),
        "factor_three": noise(seeds[2], (K, R), K ** -0.5, 0.1875, ((0, 4),), jnp.float32),
    }


def project_block(block, factor_two, factor_three):
    highest = lax.Precision.HIGHEST
    middle = jnp.einsum('ijk,jr->irk', block, factor_two, precision=highest)
    return jnp.einsum('irk,ks->irs', middle, factor_three, precision=highest)


def reference(slab, factor_two, factor_three):
    blocks = slab.reshape(N_IA, CI, J, K)
    projected = lax.map(lambda block: project_block(block, factor_two, factor_three), blocks)
    core = projected.reshape(I, R * R)
    gram = jnp.dot(core, core.T, precision=lax.Precision.HIGHEST, preferred_element_type=jnp.float32)
    return core, gram / (R * R)
```

```python
import jax
import jax.numpy as jnp
from jax import lax
from jax.sharding import Mesh, PartitionSpec as P

HI = lax.Precision.HIGHEST


def on_device(slab, factor_two, factor_three):
    rows, _, _ = slab.shape
    rank = factor_two.shape[1]
    n_b = 64
    cols = rank * rank // n_b
    first = jnp.einsum("ijk,ks->jsi", slab, factor_three, precision=HI)
    partial_value = jnp.einsum("jr,jsi->rsi", factor_two, first, precision=HI)
    chunks = partial_value.reshape(n_b, 1, cols * rows)
    got = lax.all_to_all(chunks, ("z", "c", "l"), 0, 0, tiled=True)
    own = jnp.sum(got, axis=0)
    core = own.reshape(cols, rows).T
    sent = jnp.broadcast_to(own[None], (32, 1, cols * rows))
    every = lax.all_to_all(sent, ("h", "x", "l"), 0, 0, tiled=True)
    every = every.reshape(8, 4, cols, rows)
    me = lax.axis_index(("h", "x"))
    mine = lax.dynamic_index_in_dim(every, me, 0, keepdims=False)
    terms = jnp.einsum("lci,alcm->iam", mine, every, precision=HI).reshape(rows, 8 * rows)
    other = lax.ppermute(terms, "c", [(0, 1), (1, 0)])
    terms = terms + other
    parts = lax.all_to_all(jnp.broadcast_to(terms[None], (8,) + terms.shape), "z", 0, 0, tiled=True)
    gram = jnp.sum(parts, axis=0) / (rank * rank)
    return core, gram


def solution(mesh):
    fine = Mesh(mesh.devices.reshape(2, 4, 8, 2, 4), ("h", "x", "z", "c", "l"))
    placed = (P(("h", "x"), ("z", "c"), "l"), P(("z", "c"), None), P("l", None))
    return jax.shard_map(
        on_device,
        mesh=fine,
        in_specs=placed,
        out_specs=(P(("h", "x"), ("z", "c", "l")), P(("h", "x"), None)),
        check_vma=False,
    )
```

```python
import functools
import jax
import jax.numpy as jnp
from jax import lax
from jax.experimental import pallas as pl
from jax.experimental.pallas import tpu as pltpu
from jax.sharding import Mesh, PartitionSpec as P

F32, BF16 = jnp.float32, jnp.bfloat16
NT = (((1,), (1,)), ((), ()))


def halves(x):
    high = x.astype(BF16)
    return high, (x - high.astype(F32)).astype(BF16)


def exact_nt(left, right):
    m = left.shape[0]
    lh, ll = halves(left)
    rh, rl = halves(right)
    both = lax.dot_general(jnp.concatenate([lh, ll], 0), rh, NT, preferred_element_type=F32)
    return both[:m] + both[m:] + lax.dot_general(lh, rl, NT, preferred_element_type=F32)


def project(slab_ref, two_ref, three_ref, out_ref, turned):
    step = pl.program_id(0)
    group, across, depth = slab_ref.shape
    rank = two_ref.shape[0]
    height = turned.shape[0] // rank
    first = exact_nt(three_ref[...], slab_ref[...].reshape(group * across, depth))
    for q in range(group):
        turned[pl.ds(step * group + q, rank, stride=height), :] = first[:, q * across : (q + 1) * across]

    @pl.when(step == pl.num_programs(0) - 1)
    def _():
        done = exact_nt(two_ref[...], turned[...])
        tiles = rank * height // 128
        for t in range(tiles):
            out_ref[pl.ds(t, rank, stride=tiles), :] = done[:, 128 * t : 128 * (t + 1)]


def front(slab, two, three, group=4):
    height, across, depth = slab.shape
    rank = two.shape[0]
    rows = rank * rank * height // 128
    return pl.pallas_call(
        project,
        grid=(height // group,),
        in_specs=[
            pl.BlockSpec((group, across, depth), lambda g: (g, 0, 0)),
            pl.BlockSpec((rank, across), lambda g: (0, 0)),
            pl.BlockSpec((rank, depth), lambda g: (0, 0)),
        ],
        out_specs=pl.BlockSpec((rows, 128), lambda g: (0, 0)),
        out_shape=jax.ShapeDtypeStruct((rows, 128), F32),
        scratch_shapes=[pltpu.VMEM((rank * height, across), F32)],
        name="project",
    )(slab, two, three)


def gather_sum(n_parts, copies, got_ref, core_ref, sent_ref, cols):
    rows = got_ref.shape[0] // n_parts
    own = got_ref[:rows, :]
    for b in range(1, n_parts):
        own = own + got_ref[rows * b : rows * (b + 1), :]
    for b in range(copies):
        sent_ref[rows * b : rows * (b + 1), :] = own
    height = core_ref.shape[0]
    per = 128 // height
    for q in range(per):
        cols[pl.ds(q, rows, stride=per), :] = own[:, height * q : height * (q + 1)]
    core_ref[...] = cols[...].T


def reduce_chunks(got, n_parts, copies, height):
    rows = got.shape[0] // n_parts
    n_cols = rows * 128 // height
    return pl.pallas_call(
        functools.partial(gather_sum, n_parts, copies),
        out_shape=(
            jax.ShapeDtypeStruct((height, n_cols), F32),
            jax.ShapeDtypeStruct((copies * rows, 128), F32),
        ),
        scratch_shapes=[pltpu.VMEM((n_cols, height), F32)],
        name="reduce_chunks",
    )(got)


def gram_terms(n_rows, height, axes, all_ref, out_ref):
    me = lax.axis_index(axes)
    per = 128 // height
    deep = all_ref.shape[0] // n_rows
    blocks = [all_ref[deep * a : deep * (a + 1), :] for a in range(n_rows)]
    mine = jnp.zeros_like(blocks[0])
    for a in range(n_rows):
        mine = jnp.where(me == a, blocks[a], mine)
    left = mine.T
    lane = lax.broadcasted_iota(jnp.int32, (height, 128), 1) // height
    folded = []
    for a in range(n_rows):
        z = exact_nt(left, blocks[a].T)
        u = jnp.zeros((height, 128), F32)
        for q in range(per):
            u = jnp.where(lane == q, z[height * q : height * (q + 1), :], u)
        shift = 64
        while shift >= height:
            u = u + pltpu.roll(u, shift, 1)
            shift //= 2
        folded.append(u)
    for t in range(n_rows // per):
        u = folded[t * per]
        for q in range(1, per):
            u = jnp.where(lane == q, folded[t * per + q], u)
        out_ref[:, 128 * t : 128 * (t + 1)] = u


def gram_part(every, n_rows, height, axes):
    return pl.pallas_call(
        functools.partial(gram_terms, n_rows, height, axes),
        out_shape=jax.ShapeDtypeStruct((height, n_rows * height), F32),
        name="gram_part",
    )(every)


def on_device(slab, factor_two, factor_three):
    height = slab.shape[0]
    rank = factor_two.shape[1]
    chunks = front(slab, factor_two.T, factor_three.T).reshape(64, 1, -1)
    got = lax.all_to_all(chunks, ("z", "c", "l"), 0, 0, tiled=True).reshape(-1, 128)
    core, sent = reduce_chunks(got, 64, 32, height)
    every = lax.all_to_all(sent.reshape(32, 1, -1), ("h", "x", "l"), 0, 0, tiled=True).reshape(-1, 128)
    terms = gram_part(every, 8, height, ("h", "x"))
    terms = terms + lax.ppermute(terms, "c", [(0, 1), (1, 0)])
    parts = lax.all_to_all(jnp.broadcast_to(terms[None], (8,) + terms.shape), "z", 0, 0, tiled=True)
    gram = jnp.sum(parts, axis=0) / (rank * rank)
    return core, gram


def solution(mesh):
    fine = Mesh(mesh.devices.reshape(2, 4, 8, 2, 4), ("h", "x", "z", "c", "l"))
    placed = (P(("h", "x"), ("z", "c"), "l"), P(("z", "c"), None), P("l", None))
    return jax.shard_map(
        on_device,
        mesh=fine,
        in_specs=placed,
        out_specs=(P(("h", "x"), ("z", "c", "l")), P(("h", "x"), None)),
        check_vma=False,
    )
```

```python
import functools
import jax
import jax.numpy as jnp
from jax import lax
from jax.experimental import pallas as pl
from jax.experimental.pallas import tpu as pltpu
from jax.sharding import Mesh, PartitionSpec as P

F32, BF16 = jnp.float32, jnp.bfloat16
NT = (((1,), (1,)), ((), ()))


def halves(x):
    high = x.astype(BF16)
    return high, (x - high.astype(F32)).astype(BF16)


def exact_nt(left, right):
    m = left.shape[0]
    lh, ll = halves(left)
    rh, rl = halves(right)
    both = lax.dot_general(jnp.concatenate([lh, ll], 0), rh, NT, preferred_element_type=F32)
    return both[:m] + both[m:] + lax.dot_general(lh, rl, NT, preferred_element_type=F32)


def project(slab_ref, two_ref, three_ref, out_ref, turned):
    step = pl.program_id(0)
    group, across, depth = slab_ref.shape
    rank = two_ref.shape[0]
    height = turned.shape[0] // rank
    first = exact_nt(three_ref[...], slab_ref[...].reshape(group * across, depth))
    for q in range(group):
        turned[pl.ds(step * group + q, rank, stride=height), :] = first[:, q * across : (q + 1) * across]

    @pl.when(step == pl.num_programs(0) - 1)
    def _():
        done = exact_nt(two_ref[...], turned[...])
        tiles = rank * height // 128
        for t in range(tiles):
            out_ref[pl.ds(t, rank, stride=tiles), :] = done[:, 128 * t : 128 * (t + 1)]


def front(slab, two, three, group=16):
    height, across, depth = slab.shape
    rank = two.shape[0]
    rows = rank * rank * height // 128
    return pl.pallas_call(
        project,
        grid=(height // group,),
        in_specs=[
            pl.BlockSpec((group, across, depth), lambda g: (g, 0, 0)),
            pl.BlockSpec((rank, across), lambda g: (0, 0)),
            pl.BlockSpec((rank, depth), lambda g: (0, 0)),
        ],
        out_specs=pl.BlockSpec((rows, 128), lambda g: (0, 0)),
        out_shape=pltpu.VMEM((rows, 128), F32),
        scratch_shapes=[pltpu.VMEM((rank * height, across), F32)],
        compiler_params=pltpu.CompilerParams(vmem_limit_bytes=16 << 20),
        name="project",
    )(*(pltpu.with_memory_space_constraint(x, pltpu.HBM) for x in (slab, two, three)))


def gather_sum(n_parts, copies, got_ref, core_ref, sent_ref, cols, pattern):
    rows = got_ref.shape[0] // n_parts
    wide = 8 * rows
    total = got_ref[:wide, :]
    for b in range(1, n_parts // 8):
        total = total + got_ref[wide * b : wide * (b + 1), :]
    pattern[...] = total
    own = pattern[:rows, :]
    for b in range(1, 8):
        own = own + pattern[rows * b : rows * (b + 1), :]
    for b in range(8):
        pattern[rows * b : rows * (b + 1), :] = own
    total = pattern[...]
    for b in range(copies // 8):
        sent_ref[wide * b : wide * (b + 1), :] = total
    height = core_ref.shape[0]
    per = 128 // height
    for q in range(per):
        cols[pl.ds(q, rows, stride=per), :] = own[:, height * q : height * (q + 1)]
    core_ref[...] = cols[...].T


def reduce_chunks(got, n_parts, copies, height):
    rows = got.shape[0] // n_parts
    n_cols = rows * 128 // height
    return pl.pallas_call(
        functools.partial(gather_sum, n_parts, copies),
        out_shape=(
            jax.ShapeDtypeStruct((height, n_cols), F32),
            pltpu.VMEM((copies * rows, 128), F32),
        ),
        scratch_shapes=[pltpu.VMEM((n_cols, height), F32), pltpu.VMEM((8 * rows, 128), F32)],
        compiler_params=pltpu.CompilerParams(vmem_limit_bytes=4 << 20),
        name="reduce_chunks",
    )(pltpu.with_memory_space_constraint(got, pltpu.VMEM))


def gram_terms(n_rows, height, axes, all_ref, out_ref):
    me = lax.axis_index(axes)
    per = 128 // height
    deep = all_ref.shape[0] // n_rows
    blocks = [all_ref[deep * a : deep * (a + 1), :] for a in range(n_rows)]
    mine = jnp.zeros_like(blocks[0])
    for a in range(n_rows):
        mine = jnp.where(me == a, blocks[a], mine)
    lh, ll = halves(mine.T)
    rh, rl = halves(jnp.concatenate(blocks, 1))
    both = jnp.dot(jnp.concatenate([lh, ll], 0), rh, preferred_element_type=F32)
    low = jnp.dot(lh, rl, preferred_element_type=F32)
    lane = lax.broadcasted_iota(jnp.int32, (height, 128), 1) // height
    folded = []
    for a in range(n_rows):
        z = both[:128, 128 * a : 128 * (a + 1)] + both[128:, 128 * a : 128 * (a + 1)] + low[:, 128 * a : 128 * (a + 1)]
        u = jnp.zeros((height, 128), F32)
        for q in range(per):
            u = jnp.where(lane == q, z[height * q : height * (q + 1), :], u)
        shift = 64
        while shift >= height:
            u = u + pltpu.roll(u, shift, 1)
            shift //= 2
        folded.append(u)
    for t in range(n_rows // per):
        u = folded[t * per]
        for q in range(1, per):
            u = jnp.where(lane == q, folded[t * per + q], u)
        out_ref[:, 128 * t : 128 * (t + 1)] = u


def gram_part(every, n_rows, height, axes):
    return pl.pallas_call(
        functools.partial(gram_terms, n_rows, height, axes),
        out_shape=pltpu.VMEM((height, n_rows * height), F32),
        compiler_params=pltpu.CompilerParams(vmem_limit_bytes=4 << 20),
        name="gram_part",
    )(pltpu.with_memory_space_constraint(every, pltpu.VMEM))


def on_device(slab, factor_two, factor_three):
    height = slab.shape[0]
    rank = factor_two.shape[1]
    chunks = front(slab, factor_two.T, factor_three.T).reshape(64, 1, -1)
    got = lax.all_to_all(chunks, ("z", "c", "l"), 0, 0, tiled=True).reshape(-1, 128)
    core, sent = reduce_chunks(got, 64, 32, height)
    every = lax.all_to_all(sent.reshape(32, 1, -1), ("h", "x", "l"), 0, 0, tiled=True).reshape(-1, 128)
    terms = gram_part(every, 8, height, ("h", "x"))
    terms = terms + lax.ppermute(terms, "c", [(0, 1), (1, 0)])
    parts = lax.all_to_all(jnp.broadcast_to(terms[None], (8,) + terms.shape), "z", 0, 0, tiled=True)
    gram = jnp.sum(parts, axis=0) / (rank * rank)
    return core, gram


def solution(mesh):
    fine = Mesh(mesh.devices.reshape(2, 4, 8, 2, 4), ("h", "x", "z", "c", "l"))
    placed = (P(("h", "x"), ("z", "c"), "l"), P(("z", "c"), None), P("l", None))
    return jax.shard_map(
        on_device,
        mesh=fine,
        in_specs=placed,
        out_specs=(P(("h", "x"), ("z", "c", "l")), P(("h", "x"), None)),
        check_vma=False,
    )
```

```python
import functools
import jax
import jax.numpy as jnp
from jax import lax
from jax.experimental import pallas as pl
from jax.experimental.pallas import tpu as pltpu
from jax.sharding import Mesh, PartitionSpec as P

F32, BF16 = jnp.float32, jnp.bfloat16
NT = (((1,), (1,)), ((), ()))


def halves(x):
    high = x.astype(BF16)
    return high, (x - high.astype(F32)).astype(BF16)


def exact_nt(left, right):
    m = left.shape[0]
    lh, ll = halves(left)
    rh, rl = halves(right)
    both = lax.dot_general(jnp.concatenate([lh, ll], 0), rh, NT, preferred_element_type=F32)
    return both[:m] + both[m:] + lax.dot_general(lh, rl, NT, preferred_element_type=F32)


def project(slab_ref, two_ref, three_ref, out_ref, turned):
    step = pl.program_id(0)
    group, across, depth = slab_ref.shape
    rank = two_ref.shape[0]
    height = turned.shape[0] // rank
    first = exact_nt(three_ref[...], slab_ref[...].reshape(group * across, depth))
    for q in range(group):
        turned[pl.ds(step * group + q, rank, stride=height), :] = first[:, q * across : (q + 1) * across]

    @pl.when(step == pl.num_programs(0) - 1)
    def _():
        two = two_ref[...]
        done = exact_nt(jnp.concatenate([two[r : r + 1] for r in range(rank - 1, -1, -1)], 0), turned[...])
        tiles = rank * height // 128
        for t in range(tiles):
            out_ref[pl.ds(tiles - 1 - t, rank, stride=tiles), :] = done[:, 128 * t : 128 * (t + 1)]


def front(slab, two, three, group=16):
    height, across, depth = slab.shape
    rank = two.shape[0]
    rows = rank * rank * height // 128
    return pl.pallas_call(
        project,
        grid=(height // group,),
        in_specs=[
            pl.BlockSpec((group, across, depth), lambda g: (g, 0, 0)),
            pl.BlockSpec((rank, across), lambda g: (0, 0)),
            pl.BlockSpec((rank, depth), lambda g: (0, 0)),
        ],
        out_specs=pl.BlockSpec((rows, 128), lambda g: (0, 0)),
        out_shape=pltpu.VMEM((rows, 128), F32),
        scratch_shapes=[pltpu.VMEM((rank * height, across), F32)],
        compiler_params=pltpu.CompilerParams(vmem_limit_bytes=16 << 20),
        name="project",
    )(*(pltpu.with_memory_space_constraint(x, pltpu.HBM) for x in (slab, two, three)))


def gather_sum(n_parts, copies, got_ref, core_ref, sent_ref, cols, pattern):
    rows = got_ref.shape[0] // n_parts
    wide = 8 * rows
    total = got_ref[:wide, :]
    for b in range(1, n_parts // 8):
        total = total + got_ref[wide * b : wide * (b + 1), :]
    pattern[...] = total
    own = pattern[:rows, :]
    for b in range(1, 8):
        own = own + pattern[rows * b : rows * (b + 1), :]
    for b in range(8):
        pattern[rows * b : rows * (b + 1), :] = own
    total = pattern[...]
    for b in range(copies // 8):
        sent_ref[wide * b : wide * (b + 1), :] = total
    height = core_ref.shape[0]
    per = 128 // height
    for q in range(per):
        for m in range(rows):
            at = per * (rows - 1 - m) + q
            cols[at : at + 1, :] = own[m : m + 1, height * q : height * (q + 1)]
    core_ref[...] = cols[...].T


def reduce_chunks(got, n_parts, copies, height):
    rows = got.shape[0] // n_parts
    n_cols = rows * 128 // height
    return pl.pallas_call(
        functools.partial(gather_sum, n_parts, copies),
        out_shape=(
            jax.ShapeDtypeStruct((height, n_cols), F32),
            pltpu.VMEM((copies * rows, 128), F32),
        ),
        scratch_shapes=[pltpu.VMEM((n_cols, height), F32), pltpu.VMEM((8 * rows, 128), F32)],
        compiler_params=pltpu.CompilerParams(vmem_limit_bytes=4 << 20),
        name="reduce_chunks",
    )(pltpu.with_memory_space_constraint(got, pltpu.VMEM))


def gram_terms(n_rows, height, axes, all_ref, out_ref):
    me = lax.axis_index(axes)
    per = 128 // height
    deep = all_ref.shape[0] // n_rows
    blocks = [all_ref[deep * a : deep * (a + 1), :] for a in range(n_rows)][::-1]
    mine = jnp.zeros_like(blocks[0])
    for a in range(n_rows):
        mine = jnp.where(me == a, blocks[a], mine)
    lh, ll = halves(mine.T)
    rh, rl = halves(jnp.concatenate(blocks, 1))
    both = jnp.dot(jnp.concatenate([lh, ll], 0), rh, preferred_element_type=F32)
    low = jnp.dot(lh, rl, preferred_element_type=F32)
    lane = lax.broadcasted_iota(jnp.int32, (height, 128), 1) // height
    folded = []
    for a in range(n_rows):
        z = both[:128, 128 * a : 128 * (a + 1)] + both[128:, 128 * a : 128 * (a + 1)] + low[:, 128 * a : 128 * (a + 1)]
        u = jnp.zeros((height, 128), F32)
        for q in range(per):
            u = jnp.where(lane == q, z[height * q : height * (q + 1), :], u)
        shift = 64
        while shift >= height:
            u = u + pltpu.roll(u, shift, 1)
            shift //= 2
        folded.append(u)
    for t in range(n_rows // per):
        u = folded[t * per]
        for q in range(1, per):
            u = jnp.where(lane == q, folded[t * per + q], u)
        out_ref[:, 128 * t : 128 * (t + 1)] = u


def gram_part(every, n_rows, height, axes):
    return pl.pallas_call(
        functools.partial(gram_terms, n_rows, height, axes),
        out_shape=pltpu.VMEM((height, n_rows * height), F32),
        compiler_params=pltpu.CompilerParams(vmem_limit_bytes=4 << 20),
        name="gram_part",
    )(pltpu.with_memory_space_constraint(every, pltpu.VMEM))


def on_device(slab, factor_two, factor_three):
    height = slab.shape[0]
    rank = factor_two.shape[1]
    chunks = front(slab, factor_two.T, factor_three.T).reshape(64, 1, -1)
    got = lax.all_to_all(chunks, ("z", "c", "l"), 0, 0, tiled=True, axis_index_groups=[list(range(63, -1, -1))]).reshape(-1, 128)
    core, sent = reduce_chunks(got, 64, 32, height)
    every = lax.all_to_all(sent.reshape(32, 1, -1), ("h", "x", "l"), 0, 0, tiled=True, axis_index_groups=[list(range(31, -1, -1))]).reshape(-1, 128)
    terms = gram_part(every, 8, height, ("h", "x"))
    terms = terms + lax.ppermute(terms, "c", [(0, 1), (1, 0)])
    parts = lax.all_to_all(jnp.broadcast_to(terms[None], (8,) + terms.shape), "z", 0, 0, tiled=True, axis_index_groups=[[7, 6, 5, 4, 3, 2, 1, 0]])
    gram = jnp.sum(parts, axis=0) / (rank * rank)
    return core, gram


def solution(mesh):
    fine = Mesh(mesh.devices.reshape(2, 4, 8, 2, 4), ("h", "x", "z", "c", "l"))
    placed = (P(("h", "x"), ("z", "c"), "l"), P(("z", "c"), None), P("l", None))
    return jax.shard_map(
        on_device,
        mesh=fine,
        in_specs=placed,
        out_specs=(P(("h", "x"), ("z", "c", "l")), P(("h", "x"), None)),
        check_vma=False,
    )
```

```python
import functools
import jax
import jax.numpy as jnp
from jax import lax
from jax.experimental import pallas as pl
from jax.experimental.pallas import tpu as pltpu
from jax.sharding import Mesh, PartitionSpec as P

F32, BF16 = jnp.float32, jnp.bfloat16
NT = (((1,), (1,)), ((), ()))


def halves(x):
    high = x.astype(BF16)
    return high, (x - high.astype(F32)).astype(BF16)


def exact_nt(left, right):
    m = left.shape[0]
    lh, ll = halves(left)
    rh, rl = halves(right)
    both = lax.dot_general(jnp.concatenate([lh, ll], 0), rh, NT, preferred_element_type=F32)
    return both[:m] + both[m:] + lax.dot_general(lh, rl, NT, preferred_element_type=F32)


def project(slab_ref, two_ref, three_ref, out_ref, turned):
    step = pl.program_id(0)
    group, across, depth = slab_ref.shape
    rank = two_ref.shape[0]
    height = turned.shape[0] // rank
    first = exact_nt(three_ref[...], slab_ref[...].reshape(group * across, depth))
    for q in range(group):
        turned[pl.ds(step * group + q, rank, stride=height), :] = first[:, q * across : (q + 1) * across]

    @pl.when(step == pl.num_programs(0) - 1)
    def _():
        two = two_ref[...]
        done = exact_nt(jnp.concatenate([two[r : r + 1] for r in range(rank - 1, -1, -1)], 0), turned[...])
        tiles = rank * height // 128
        for t in range(tiles):
            out_ref[pl.ds(tiles - 1 - t, rank, stride=tiles), :] = done[:, 128 * t : 128 * (t + 1)]


def front(slab, two, three, group=16):
    height, across, depth = slab.shape
    rank = two.shape[0]
    rows = rank * rank * height // 128
    return pl.pallas_call(
        project,
        grid=(height // group,),
        in_specs=[
            pl.BlockSpec((group, across, depth), lambda g: (g, 0, 0)),
            pl.BlockSpec((rank, across), lambda g: (0, 0)),
            pl.BlockSpec((rank, depth), lambda g: (0, 0)),
        ],
        out_specs=pl.BlockSpec((rows, 128), lambda g: (0, 0)),
        out_shape=pltpu.VMEM((rows, 128), F32),
        scratch_shapes=[pltpu.VMEM((rank * height, across), F32)],
        compiler_params=pltpu.CompilerParams(vmem_limit_bytes=16 << 20),
        name="project",
    )(*(pltpu.with_memory_space_constraint(x, pltpu.HBM) for x in (slab, two, three)))


def gather_sum(n_parts, copies, got_ref, sent_ref, pattern):
    rows = got_ref.shape[0] // n_parts
    wide = 8 * rows
    total = got_ref[:wide, :]
    for b in range(1, n_parts // 8):
        total = total + got_ref[wide * b : wide * (b + 1), :]
    pattern[...] = total
    own = pattern[:rows, :]
    for b in range(1, 8):
        own = own + pattern[rows * b : rows * (b + 1), :]
    for b in range(8):
        pattern[rows * b : rows * (b + 1), :] = own
    total = pattern[...]
    for b in range(copies // 8):
        sent_ref[wide * b : wide * (b + 1), :] = total


def format_core(sent_ref, core_ref, cols):
    height, n_cols = core_ref.shape
    per = 128 // height
    rows = n_cols // per
    own = sent_ref[:rows, :]
    for q in range(per):
        for m in range(rows):
            at = per * (rows - 1 - m) + q
            cols[at : at + 1, :] = own[m : m + 1, height * q : height * (q + 1)]
    core_ref[...] = cols[...].T


def core_block(sent, height, n_cols):
    return pl.pallas_call(
        format_core,
        out_shape=jax.ShapeDtypeStruct((height, n_cols), F32),
        scratch_shapes=[pltpu.VMEM((n_cols, height), F32)],
        compiler_params=pltpu.CompilerParams(vmem_limit_bytes=4 << 20),
        cost_estimate=pl.CostEstimate(flops=1 << 20, bytes_accessed=1 << 21, transcendentals=0),
        name="core_block",
    )(pltpu.with_memory_space_constraint(sent, pltpu.VMEM))


def reduce_chunks(got, n_parts, copies):
    rows = got.shape[0] // n_parts
    return pl.pallas_call(
        functools.partial(gather_sum, n_parts, copies),
        out_shape=pltpu.VMEM((copies * rows, 128), F32),
        scratch_shapes=[pltpu.VMEM((8 * rows, 128), F32)],
        compiler_params=pltpu.CompilerParams(vmem_limit_bytes=4 << 20),
        name="reduce_chunks",
    )(pltpu.with_memory_space_constraint(got, pltpu.VMEM))


def gram_terms(n_rows, height, axes, all_ref, out_ref):
    me = lax.axis_index(axes)
    per = 128 // height
    deep = all_ref.shape[0] // n_rows
    blocks = [all_ref[deep * a : deep * (a + 1), :] for a in range(n_rows)][::-1]
    mine = jnp.zeros_like(blocks[0])
    for a in range(n_rows):
        mine = jnp.where(me == a, blocks[a], mine)
    lh, ll = halves(mine.T)
    rh, rl = halves(jnp.concatenate(blocks, 1))
    both = jnp.dot(jnp.concatenate([lh, ll], 0), rh, preferred_element_type=F32)
    low = jnp.dot(lh, rl, preferred_element_type=F32)
    lane = lax.broadcasted_iota(jnp.int32, (height, 128), 1) // height
    folded = []
    for a in range(n_rows):
        z = both[:128, 128 * a : 128 * (a + 1)] + both[128:, 128 * a : 128 * (a + 1)] + low[:, 128 * a : 128 * (a + 1)]
        u = jnp.zeros((height, 128), F32)
        for q in range(per):
            u = jnp.where(lane == q, z[height * q : height * (q + 1), :], u)
        shift = 64
        while shift >= height:
            u = u + pltpu.roll(u, shift, 1)
            shift //= 2
        folded.append(u)
    for t in range(n_rows // per):
        u = folded[t * per]
        for q in range(1, per):
            u = jnp.where(lane == q, folded[t * per + q], u)
        out_ref[:, 128 * t : 128 * (t + 1)] = u


def gram_part(every, n_rows, height, axes):
    return pl.pallas_call(
        functools.partial(gram_terms, n_rows, height, axes),
        out_shape=pltpu.VMEM((height, n_rows * height), F32),
        compiler_params=pltpu.CompilerParams(vmem_limit_bytes=4 << 20),
        name="gram_part",
    )(pltpu.with_memory_space_constraint(every, pltpu.VMEM))


def on_device(slab, factor_two, factor_three):
    height = slab.shape[0]
    rank = factor_two.shape[1]
    chunks = front(slab, factor_two.T, factor_three.T).reshape(64, 1, -1)
    got = lax.all_to_all(chunks, ("z", "c", "l"), 0, 0, tiled=True, axis_index_groups=[list(range(63, -1, -1))]).reshape(-1, 128)
    sent = reduce_chunks(got, 64, 32)
    every = lax.all_to_all(sent.reshape(32, 1, -1), ("h", "x", "l"), 0, 0, tiled=True, axis_index_groups=[list(range(31, -1, -1))]).reshape(-1, 128)
    terms = gram_part(every, 8, height, ("h", "x"))
    core = core_block(sent, height, rank * rank // 64)
    other = lax.ppermute(terms, "c", [(0, 1), (1, 0)])
    terms, other, core = lax.optimization_barrier((terms, other, core))
    terms = terms + other
    parts = lax.all_to_all(jnp.broadcast_to(terms[None], (8,) + terms.shape), "z", 0, 0, tiled=True, axis_index_groups=[[7, 5, 6, 4, 3, 2, 1, 0]])
    gram = jnp.sum(parts, axis=0) / (rank * rank)
    return core, gram


def solution(mesh):
    fine = Mesh(mesh.devices.reshape(2, 4, 8, 2, 4), ("h", "x", "z", "c", "l"))
    placed = (P(("h", "x"), ("z", "c"), "l"), P(("z", "c"), None), P("l", None))
    return jax.shard_map(
        on_device,
        mesh=fine,
        in_specs=placed,
        out_specs=(P(("h", "x"), ("z", "c", "l")), P(("h", "x"), None)),
        check_vma=False,
    )
```

```python
import functools
import jax
import jax.numpy as jnp
from jax import lax
from jax.experimental import pallas as pl
from jax.experimental.pallas import tpu as pltpu
from jax.sharding import Mesh, PartitionSpec as P

F32, BF16 = jnp.float32, jnp.bfloat16
NT = (((1,), (1,)), ((), ()))


def halves(x):
    high = x.astype(BF16)
    return high, (x - high.astype(F32)).astype(BF16)


def exact_nt(left, right):
    m = left.shape[0]
    lh, ll = halves(left)
    rh, rl = halves(right)
    both = lax.dot_general(jnp.concatenate([lh, ll], 0), rh, NT, preferred_element_type=F32)
    return both[:m] + both[m:] + lax.dot_general(lh, rl, NT, preferred_element_type=F32)


def project(slab_ref, two_ref, three_ref, out_ref, turned):
    step = pl.program_id(0)
    group, across, depth = slab_ref.shape
    rank = two_ref.shape[0]
    height = turned.shape[0] // rank
    first = exact_nt(three_ref[...], slab_ref[...].reshape(group * across, depth))
    for q in range(group):
        turned[pl.ds(step * group + q, rank, stride=height), :] = first[:, q * across : (q + 1) * across]

    @pl.when(step == pl.num_programs(0) - 1)
    def _():
        two = two_ref[...]
        turns = [two[r : r + 1] for c in range(2) for r in range(rank - 1, -1, -1) if r // 3 % 2 == c]
        done = exact_nt(jnp.concatenate(turns, 0), turned[...])
        half, tiles = rank // 2, rank * height // 128
        for c in range(2):
            for t in range(tiles):
                piece = done[half * c : half * (c + 1), 128 * t : 128 * (t + 1)]
                out_ref[pl.ds(half * tiles * c + tiles - 1 - t, half, stride=tiles), :] = piece


def front(slab, two, three, group=16):
    height, across, depth = slab.shape
    rank = two.shape[0]
    rows = rank * rank * height // 128
    return pl.pallas_call(
        project,
        grid=(height // group,),
        in_specs=[
            pl.BlockSpec((group, across, depth), lambda g: (g, 0, 0)),
            pl.BlockSpec((rank, across), lambda g: (0, 0)),
            pl.BlockSpec((rank, depth), lambda g: (0, 0)),
        ],
        out_specs=pl.BlockSpec((rows, 128), lambda g: (0, 0)),
        out_shape=pltpu.VMEM((rows, 128), F32),
        scratch_shapes=[pltpu.VMEM((rank * height, across), F32)],
        compiler_params=pltpu.CompilerParams(vmem_limit_bytes=16 << 20),
        name="project",
    )(*(pltpu.with_memory_space_constraint(x, pltpu.HBM) for x in (slab, two, three)))


def gather_sum(n_parts, copies, got_ref, sent_ref, pattern):
    rows = got_ref.shape[0] // n_parts
    wide = 8 * rows
    total = got_ref[:wide, :]
    for b in range(1, n_parts // 8):
        total = total + got_ref[wide * b : wide * (b + 1), :]
    pattern[...] = total
    own = pattern[:rows, :]
    for b in range(1, 8):
        own = own + pattern[rows * b : rows * (b + 1), :]
    for b in range(8):
        pattern[rows * b : rows * (b + 1), :] = own
    total = pattern[...]
    for b in range(copies // 8):
        sent_ref[wide * b : wide * (b + 1), :] = total


def finish_all(scale, parts_ref, sent_ref, gram_ref, core_ref, cols):
    n_parts = parts_ref.shape[0]
    total = parts_ref[0]
    for b in range(1, n_parts):
        total = total + parts_ref[b]
    gram_ref[...] = total * scale
    height, n_cols = core_ref.shape
    per = 128 // height
    rows = n_cols // per
    own = sent_ref[:rows, :]
    for q in range(per):
        for m in range(rows):
            at = per * (rows - 1 - m) + q
            cols[at : at + 1, :] = own[m : m + 1, height * q : height * (q + 1)]
    core_ref[...] = cols[...].T


def finish(parts, sent, n_cols, scale):
    height, width = parts.shape[1:]
    return pl.pallas_call(
        functools.partial(finish_all, scale),
        out_shape=(jax.ShapeDtypeStruct((height, width), F32), jax.ShapeDtypeStruct((height, n_cols), F32)),
        scratch_shapes=[pltpu.VMEM((n_cols, height), F32)],
        compiler_params=pltpu.CompilerParams(vmem_limit_bytes=4 << 20),
        name="finish",
    )(*(pltpu.with_memory_space_constraint(x, pltpu.VMEM) for x in (parts, sent)))


def reduce_chunks(got, n_parts, copies):
    rows = got.shape[0] // n_parts
    return pl.pallas_call(
        functools.partial(gather_sum, n_parts, copies),
        out_shape=pltpu.VMEM((copies * rows, 128), F32),
        scratch_shapes=[pltpu.VMEM((8 * rows, 128), F32)],
        compiler_params=pltpu.CompilerParams(vmem_limit_bytes=4 << 20),
        name="reduce_chunks",
    )(pltpu.with_memory_space_constraint(got, pltpu.VMEM))


def gram_terms(n_rows, height, axes, all_ref, out_ref):
    me = lax.axis_index(axes)
    per = 128 // height
    deep = all_ref.shape[0] // n_rows
    blocks = [all_ref[deep * a : deep * (a + 1), :] for a in range(n_rows)][::-1]
    mine = jnp.zeros_like(blocks[0])
    for a in range(n_rows):
        mine = jnp.where(me == a, blocks[a], mine)
    lh, ll = halves(mine.T)
    rh, rl = halves(jnp.concatenate(blocks, 1))
    both = jnp.dot(jnp.concatenate([lh, ll], 0), rh, preferred_element_type=F32)
    low = jnp.dot(lh, rl, preferred_element_type=F32)
    lane = lax.broadcasted_iota(jnp.int32, (height, 128), 1) // height
    folded = []
    for a in range(n_rows):
        z = both[:128, 128 * a : 128 * (a + 1)] + both[128:, 128 * a : 128 * (a + 1)] + low[:, 128 * a : 128 * (a + 1)]
        u = jnp.zeros((height, 128), F32)
        for q in range(per):
            u = jnp.where(lane == q, z[height * q : height * (q + 1), :], u)
        shift = 64
        while shift >= height:
            u = u + pltpu.roll(u, shift, 1)
            shift //= 2
        folded.append(u)
    for t in range(n_rows // per):
        u = folded[t * per]
        for q in range(1, per):
            u = jnp.where(lane == q, folded[t * per + q], u)
        out_ref[:, 128 * t : 128 * (t + 1)] = u


def gram_part(every, n_rows, height, axes):
    return pl.pallas_call(
        functools.partial(gram_terms, n_rows, height, axes),
        out_shape=pltpu.VMEM((height, n_rows * height), F32),
        compiler_params=pltpu.CompilerParams(vmem_limit_bytes=4 << 20),
        name="gram_part",
    )(pltpu.with_memory_space_constraint(every, pltpu.VMEM))


def add_half(axis, both_ref, out_ref):
    rows = out_ref.shape[0]
    first = both_ref[0, :rows, :] + both_ref[1, :rows, :]
    second = both_ref[0, rows:, :] + both_ref[1, rows:, :]
    out_ref[...] = jnp.where(lax.axis_index(axis) == 0, first, second)


def core_sum(both, axis):
    return pl.pallas_call(
        functools.partial(add_half, axis),
        out_shape=pltpu.VMEM((both.shape[1] // 2, 128), F32),
        compiler_params=pltpu.CompilerParams(vmem_limit_bytes=4 << 20),
        name="core_sum",
    )(pltpu.with_memory_space_constraint(both, pltpu.VMEM))


def spread_sum(pair_ref, out_ref):
    total = pair_ref[0] + pair_ref[1]
    for b in range(out_ref.shape[0]):
        out_ref[b] = total


def pair_spread(pair, copies):
    return pl.pallas_call(
        spread_sum,
        out_shape=pltpu.VMEM((copies,) + pair.shape[1:], F32),
        compiler_params=pltpu.CompilerParams(vmem_limit_bytes=4 << 20),
        name="pair_spread",
    )(pltpu.with_memory_space_constraint(pair, pltpu.VMEM))


def on_device(slab, factor_two, factor_three):
    height = slab.shape[0]
    rank = factor_two.shape[1]
    both = lax.all_gather(front(slab, factor_two.T, factor_three.T), "c", axis=0, tiled=False)
    chunks = core_sum(both, "c").reshape(32, 1, -1)
    down = list(range(31, -1, -1))
    got = lax.all_to_all(chunks, ("z", "l"), 0, 0, tiled=True, axis_index_groups=[down]).reshape(-1, 128)
    sent = reduce_chunks(got, 32, 32)
    every = lax.all_to_all(sent.reshape(32, 1, -1), ("h", "x", "l"), 0, 0, tiled=True, axis_index_groups=[down])
    terms = gram_part(every.reshape(-1, 128), 8, height, ("h", "x"))
    terms = pair_spread(lax.all_gather(terms, "c", axis=0, tiled=False), 8)
    parts = lax.all_to_all(terms, "z", 0, 0, tiled=True, axis_index_groups=[[7, 5, 6, 4, 3, 2, 1, 0]])
    gram, core = finish(parts, sent, rank * rank // 64, 1.0 / (rank * rank))
    return core, gram


def solution(mesh):
    fine = Mesh(mesh.devices.reshape(2, 4, 8, 2, 4), ("h", "x", "z", "c", "l"))
    placed = (P(("h", "x"), ("z", "c"), "l"), P(("z", "c"), None), P("l", None))
    return jax.shard_map(
        on_device,
        mesh=fine,
        in_specs=placed,
        out_specs=(P(("h", "x"), ("z", "c", "l")), P(("h", "x"), None)),
        check_vma=False,
    )
```

```python
import functools
import jax
import jax.numpy as jnp
from jax import lax
from jax.experimental import pallas as pl
from jax.experimental.pallas import tpu as pltpu
from jax.sharding import Mesh, PartitionSpec as P

F32, BF16 = jnp.float32, jnp.bfloat16
NT = (((1,), (1,)), ((), ()))


def halves(x):
    high = x.astype(BF16)
    return high, (x - high.astype(F32)).astype(BF16)


def rounded(x):
    high = x.astype(BF16).astype(F32)
    return high, x - high


def exact_nt(left, right):
    m = left.shape[0]
    lh, ll = halves(left)
    rh, rl = halves(right)
    both = lax.dot_general(jnp.concatenate([lh, ll], 0), rh, NT, preferred_element_type=F32)
    return both[:m] + both[m:] + lax.dot_general(lh, rl, NT, preferred_element_type=F32)


def project(slab_ref, two_ref, three_ref, out_ref, turned):
    step = pl.program_id(0)
    group, across, depth = slab_ref.shape
    rank = two_ref.shape[0]
    height = turned.shape[0] // rank
    first = exact_nt(three_ref[...], slab_ref[...].reshape(group * across, depth))
    for q in range(group):
        turned[pl.ds(step * group + q, rank, stride=height), :] = first[:, q * across : (q + 1) * across]

    @pl.when(step == pl.num_programs(0) - 1)
    def _():
        two = two_ref[...]
        turns = [two[r : r + 1] for c in range(2) for r in range(rank - 1, -1, -1) if r // 3 % 2 == c]
        done = exact_nt(jnp.concatenate(turns, 0), turned[...])
        half, tiles = rank // 2, rank * height // 128
        for c in range(2):
            for t in range(tiles):
                piece = done[half * c : half * (c + 1), 128 * t : 128 * (t + 1)]
                out_ref[pl.ds(half * tiles * c + tiles - 1 - t, half, stride=tiles), :] = piece


def front(slab, two, three, group=16):
    height, across, depth = slab.shape
    rank = two.shape[0]
    rows = rank * rank * height // 128
    return pl.pallas_call(
        project,
        grid=(height // group,),
        in_specs=[
            pl.BlockSpec((group, across, depth), lambda g: (g, 0, 0)),
            pl.BlockSpec((rank, across), lambda g: (0, 0)),
            pl.BlockSpec((rank, depth), lambda g: (0, 0)),
        ],
        out_specs=pl.BlockSpec((rows, 128), lambda g: (0, 0)),
        out_shape=pltpu.VMEM((rows, 128), F32),
        scratch_shapes=[pltpu.VMEM((rank * height, across), F32)],
        compiler_params=pltpu.CompilerParams(vmem_limit_bytes=16 << 20),
        name="project",
    )(*(pltpu.with_memory_space_constraint(x, pltpu.HBM) for x in (slab, two, three)))


def gather_sum(n_parts, copies, got_ref, sent_ref, pattern):
    rows = got_ref.shape[0] // n_parts
    wide = 8 * rows
    total = got_ref[:wide, :]
    for b in range(1, n_parts // 8):
        total = total + got_ref[wide * b : wide * (b + 1), :]
    pattern[...] = total
    own = pattern[:rows, :]
    for b in range(1, 8):
        own = own + pattern[rows * b : rows * (b + 1), :]
    for b in range(8):
        pattern[rows * b : rows * (b + 1), :] = own
    total = pattern[...]
    for b in range(copies // 8):
        sent_ref[wide * b : wide * (b + 1), :] = total


def finish_all(scale, parts_ref, sent_ref, gram_ref, core_ref, cols):
    n_parts = parts_ref.shape[0]
    total = parts_ref[0]
    for b in range(1, n_parts):
        total = total + parts_ref[b]
    gram_ref[...] = total * scale
    height, n_cols = core_ref.shape
    per = 128 // height
    rows = n_cols // per
    own = sent_ref[:rows, :]
    for q in range(per):
        for m in range(rows):
            at = per * (rows - 1 - m) + q
            cols[at : at + 1, :] = own[m : m + 1, height * q : height * (q + 1)]
    core_ref[...] = cols[...].T


def finish(parts, sent, n_cols, scale):
    height, width = parts.shape[1:]
    return pl.pallas_call(
        functools.partial(finish_all, scale),
        out_shape=(jax.ShapeDtypeStruct((height, width), F32), jax.ShapeDtypeStruct((height, n_cols), F32)),
        scratch_shapes=[pltpu.VMEM((n_cols, height), F32)],
        compiler_params=pltpu.CompilerParams(vmem_limit_bytes=4 << 20),
        name="finish",
    )(*(pltpu.with_memory_space_constraint(x, pltpu.VMEM) for x in (parts, sent)))


def reduce_chunks(got, n_parts, copies):
    rows = got.shape[0] // n_parts
    return pl.pallas_call(
        functools.partial(gather_sum, n_parts, copies),
        out_shape=pltpu.VMEM((copies * rows, 128), F32),
        scratch_shapes=[pltpu.VMEM((8 * rows, 128), F32)],
        compiler_params=pltpu.CompilerParams(vmem_limit_bytes=4 << 20),
        name="reduce_chunks",
    )(pltpu.with_memory_space_constraint(got, pltpu.VMEM))


def gram_terms(n_rows, height, axes, all_ref, out_ref):
    me = lax.axis_index(axes)
    per = 128 // height
    deep = all_ref.shape[0] // n_rows
    blocks = [all_ref[deep * a : deep * (a + 1), :] for a in range(n_rows)][::-1]
    mine = jnp.zeros_like(blocks[0])
    for a in range(n_rows):
        mine = jnp.where(me == a, blocks[a], mine)
    lh, ll = rounded(mine)
    rh, rl = rounded(jnp.concatenate(blocks, 1))
    gap = jnp.zeros((-deep % 8, 128), F32)
    left = jnp.concatenate([lh, gap, ll, gap, lh, gap], 0).T.astype(BF16)
    gap = jnp.zeros((-deep % 8, rh.shape[1]), F32)
    right = jnp.concatenate([rh, gap, rh, gap, rl, gap], 0).astype(BF16)
    both = jnp.dot(left, right, preferred_element_type=F32)
    lane = lax.broadcasted_iota(jnp.int32, (height, 128), 1) // height
    folded = []
    for a in range(n_rows):
        z = both[:, 128 * a : 128 * (a + 1)]
        u = jnp.zeros((height, 128), F32)
        for q in range(per):
            u = jnp.where(lane == q, z[height * q : height * (q + 1), :], u)
        shift = 64
        while shift >= height:
            u = u + pltpu.roll(u, shift, 1)
            shift //= 2
        folded.append(u)
    for t in range(n_rows // per):
        u = folded[t * per]
        for q in range(1, per):
            u = jnp.where(lane == q, folded[t * per + q], u)
        out_ref[:, 128 * t : 128 * (t + 1)] = u


def gram_part(every, n_rows, height, axes):
    return pl.pallas_call(
        functools.partial(gram_terms, n_rows, height, axes),
        out_shape=pltpu.VMEM((height, n_rows * height), F32),
        compiler_params=pltpu.CompilerParams(vmem_limit_bytes=4 << 20),
        name="gram_part",
    )(pltpu.with_memory_space_constraint(every, pltpu.VMEM))


def add_half(axis, both_ref, out_ref):
    rows = out_ref.shape[0]
    first = both_ref[0, :rows, :] + both_ref[1, :rows, :]
    second = both_ref[0, rows:, :] + both_ref[1, rows:, :]
    out_ref[...] = jnp.where(lax.axis_index(axis) == 0, first, second)


def core_sum(both, axis):
    return pl.pallas_call(
        functools.partial(add_half, axis),
        out_shape=pltpu.VMEM((both.shape[1] // 2, 128), F32),
        compiler_params=pltpu.CompilerParams(vmem_limit_bytes=4 << 20),
        name="core_sum",
    )(pltpu.with_memory_space_constraint(both, pltpu.VMEM))


def spread_sum(pair_ref, out_ref):
    total = pair_ref[0] + pair_ref[1]
    for b in range(out_ref.shape[0]):
        out_ref[b] = total


def pair_spread(pair, copies):
    return pl.pallas_call(
        spread_sum,
        out_shape=pltpu.VMEM((copies,) + pair.shape[1:], F32),
        compiler_params=pltpu.CompilerParams(vmem_limit_bytes=4 << 20),
        name="pair_spread",
    )(pltpu.with_memory_space_constraint(pair, pltpu.VMEM))


def on_device(slab, factor_two, factor_three):
    height = slab.shape[0]
    rank = factor_two.shape[1]
    both = lax.all_gather(front(slab, factor_two.T, factor_three.T), "c", axis=0, tiled=False)
    chunks = core_sum(both, "c").reshape(32, 1, -1)
    down = list(range(31, -1, -1))
    got = lax.all_to_all(chunks, ("z", "l"), 0, 0, tiled=True, axis_index_groups=[down]).reshape(-1, 128)
    sent = reduce_chunks(got, 32, 32)
    every = lax.all_to_all(sent.reshape(32, 1, -1), ("h", "x", "l"), 0, 0, tiled=True, axis_index_groups=[down])
    terms = gram_part(every.reshape(-1, 128), 8, height, ("h", "x"))
    terms = pair_spread(lax.all_gather(terms, "c", axis=0, tiled=False), 8)
    parts = lax.all_to_all(terms, "z", 0, 0, tiled=True, axis_index_groups=[[6, 7, 5, 4, 2, 3, 1, 0]])
    gram, core = finish(parts, sent, rank * rank // 64, 1.0 / (rank * rank))
    return core, gram


def solution(mesh):
    fine = Mesh(mesh.devices.reshape(2, 4, 8, 2, 4), ("h", "x", "z", "c", "l"))
    placed = (P(("h", "x"), ("z", "c"), "l"), P(("z", "c"), None), P("l", None))
    return jax.shard_map(
        on_device,
        mesh=fine,
        in_specs=placed,
        out_specs=(P(("h", "x"), ("z", "c", "l")), P(("h", "x"), None)),
        check_vma=False,
    )
```

```python
import functools
import jax
import jax.numpy as jnp
from jax import lax
from jax.experimental import pallas as pl
from jax.experimental.pallas import tpu as pltpu
from jax.sharding import Mesh, PartitionSpec as P

F32, BF16 = jnp.float32, jnp.bfloat16
NT = (((1,), (1,)), ((), ()))
SECOND = (7, 6, 5, 4, 3, 2, 1, 0)


def halves(x):
    high = x.astype(BF16)
    return high, (x - high.astype(F32)).astype(BF16)


def rounded(x):
    high = x.astype(BF16).astype(F32)
    return high, x - high


def exact_nt(left, right):
    m = left.shape[0]
    lh, ll = halves(left)
    rh, rl = halves(right)
    both = lax.dot_general(jnp.concatenate([lh, ll], 0), rh, NT, preferred_element_type=F32)
    return both[:m] + both[m:] + lax.dot_general(lh, rl, NT, preferred_element_type=F32)


def project(slab_ref, two_ref, three_ref, out_ref, turned):
    step = pl.program_id(0)
    group, across, depth = slab_ref.shape
    rank = two_ref.shape[0]
    height = turned.shape[0] // rank
    first = exact_nt(three_ref[...], slab_ref[...].reshape(group * across, depth))
    for q in range(group):
        turned[pl.ds(step * group + q, rank, stride=height), :] = first[:, q * across : (q + 1) * across]

    @pl.when(step == pl.num_programs(0) - 1)
    def _():
        two = two_ref[...]
        turns = [two[r : r + 1] for c in range(2) for r in range(rank - 1, -1, -1) if r // 3 % 2 == c]
        done = exact_nt(jnp.concatenate(turns, 0), turned[...])
        half, tiles = rank // 2, rank * height // 128
        for c in range(2):
            for t in range(tiles):
                piece = done[half * c : half * (c + 1), 128 * t : 128 * (t + 1)]
                out_ref[pl.ds(half * tiles * c + tiles - 1 - t, half, stride=tiles), :] = piece


def front(slab, two, three, group=16):
    height, across, depth = slab.shape
    rank = two.shape[0]
    rows = rank * rank * height // 128
    return pl.pallas_call(
        project,
        grid=(height // group,),
        in_specs=[
            pl.BlockSpec((group, across, depth), lambda g: (g, 0, 0)),
            pl.BlockSpec((rank, across), lambda g: (0, 0)),
            pl.BlockSpec((rank, depth), lambda g: (0, 0)),
        ],
        out_specs=pl.BlockSpec((rows, 128), lambda g: (0, 0)),
        out_shape=pltpu.VMEM((rows, 128), F32),
        scratch_shapes=[pltpu.VMEM((rank * height, across), F32)],
        compiler_params=pltpu.CompilerParams(vmem_limit_bytes=16 << 20),
        name="project",
    )(*(pltpu.with_memory_space_constraint(x, pltpu.HBM) for x in (slab, two, three)))


def gather_sum(n_parts, copies, got_ref, sent_ref, pattern):
    rows = got_ref.shape[0] // n_parts
    wide = 8 * rows
    total = got_ref[:wide, :]
    for b in range(1, n_parts // 8):
        total = total + got_ref[wide * b : wide * (b + 1), :]
    pattern[...] = total
    own = pattern[:rows, :]
    for b in range(1, 8):
        own = own + pattern[rows * b : rows * (b + 1), :]
    for b in range(8):
        pattern[rows * b : rows * (b + 1), :] = own
    total = pattern[...]
    for b in range(copies // 8):
        sent_ref[wide * b : wide * (b + 1), :] = total


def finish_all(scale, parts_ref, sent_ref, gram_ref, core_ref, cols):
    n_parts = parts_ref.shape[0]
    total = parts_ref[0]
    for b in range(1, n_parts):
        total = total + parts_ref[b]
    gram_ref[...] = total * scale
    height, n_cols = core_ref.shape
    per = 128 // height
    rows = n_cols // per
    own = sent_ref[:rows, :]
    for q in range(per):
        for m in range(rows):
            at = per * (rows - 1 - m) + q
            cols[at : at + 1, :] = own[m : m + 1, height * q : height * (q + 1)]
    core_ref[...] = cols[...].T


def finish(parts, sent, n_cols, scale):
    height, width = parts.shape[1:]
    return pl.pallas_call(
        functools.partial(finish_all, scale),
        out_shape=(jax.ShapeDtypeStruct((height, width), F32), jax.ShapeDtypeStruct((height, n_cols), F32)),
        scratch_shapes=[pltpu.VMEM((n_cols, height), F32)],
        compiler_params=pltpu.CompilerParams(vmem_limit_bytes=4 << 20),
        name="finish",
    )(*(pltpu.with_memory_space_constraint(x, pltpu.VMEM) for x in (parts, sent)))


def reduce_chunks(got, n_parts, copies):
    rows = got.shape[0] // n_parts
    return pl.pallas_call(
        functools.partial(gather_sum, n_parts, copies),
        out_shape=pltpu.VMEM((copies * rows, 128), F32),
        scratch_shapes=[pltpu.VMEM((8 * rows, 128), F32)],
        compiler_params=pltpu.CompilerParams(vmem_limit_bytes=4 << 20),
        name="reduce_chunks",
    )(pltpu.with_memory_space_constraint(got, pltpu.VMEM))


def gram_terms(n_rows, height, axes, all_ref, out_ref):
    me = lax.axis_index(axes)
    per = 128 // height
    deep = all_ref.shape[0] // n_rows
    at = [deep * SECOND.index(a) for a in range(n_rows)]
    blocks = [all_ref[s : s + deep, :] for s in at]
    piece = deep // 4
    for a in range(4, n_rows):
        blocks[a] = jnp.concatenate([blocks[a][piece * l : piece * (l + 1), :] for l in (3, 2, 1, 0)], 0)
    mine = jnp.zeros_like(blocks[0])
    for a in range(n_rows):
        mine = jnp.where(me == a, blocks[a], mine)
    lh, ll = rounded(mine)
    rh, rl = rounded(jnp.concatenate(blocks, 1))
    gap = jnp.zeros((-deep % 8, 128), F32)
    left = jnp.concatenate([lh, gap, ll, gap, lh, gap], 0).T.astype(BF16)
    gap = jnp.zeros((-deep % 8, rh.shape[1]), F32)
    right = jnp.concatenate([rh, gap, rh, gap, rl, gap], 0).astype(BF16)
    both = jnp.dot(left, right, preferred_element_type=F32)
    lane = lax.broadcasted_iota(jnp.int32, (height, 128), 1) // height
    folded = []
    for a in range(n_rows):
        z = both[:, 128 * a : 128 * (a + 1)]
        u = jnp.zeros((height, 128), F32)
        for q in range(per):
            u = jnp.where(lane == q, z[height * q : height * (q + 1), :], u)
        shift = 64
        while shift >= height:
            u = u + pltpu.roll(u, shift, 1)
            shift //= 2
        folded.append(u)
    for t in range(n_rows // per):
        u = folded[t * per]
        for q in range(1, per):
            u = jnp.where(lane == q, folded[t * per + q], u)
        out_ref[:, 128 * t : 128 * (t + 1)] = u


def gram_part(every, n_rows, height, axes):
    return pl.pallas_call(
        functools.partial(gram_terms, n_rows, height, axes),
        out_shape=pltpu.VMEM((height, n_rows * height), F32),
        compiler_params=pltpu.CompilerParams(vmem_limit_bytes=4 << 20),
        name="gram_part",
    )(pltpu.with_memory_space_constraint(every, pltpu.VMEM))


def add_half(axis, both_ref, out_ref):
    rows = out_ref.shape[0]
    first = both_ref[0, :rows, :] + both_ref[1, :rows, :]
    second = both_ref[0, rows:, :] + both_ref[1, rows:, :]
    out_ref[...] = jnp.where(lax.axis_index(axis) == 0, first, second)


def core_sum(both, axis):
    return pl.pallas_call(
        functools.partial(add_half, axis),
        out_shape=pltpu.VMEM((both.shape[1] // 2, 128), F32),
        compiler_params=pltpu.CompilerParams(vmem_limit_bytes=4 << 20),
        name="core_sum",
    )(pltpu.with_memory_space_constraint(both, pltpu.VMEM))


def spread_sum(pair_ref, out_ref):
    total = pair_ref[0] + pair_ref[1]
    for b in range(out_ref.shape[0]):
        out_ref[b] = total


def pair_spread(pair, copies):
    return pl.pallas_call(
        spread_sum,
        out_shape=pltpu.VMEM((copies,) + pair.shape[1:], F32),
        compiler_params=pltpu.CompilerParams(vmem_limit_bytes=4 << 20),
        name="pair_spread",
    )(pltpu.with_memory_space_constraint(pair, pltpu.VMEM))


def on_device(slab, factor_two, factor_three):
    height = slab.shape[0]
    rank = factor_two.shape[1]
    both = lax.all_gather(front(slab, factor_two.T, factor_three.T), "c", axis=0, tiled=False)
    chunks = core_sum(both, "c").reshape(32, 1, -1)
    down = list(range(31, -1, -1))
    got = lax.all_to_all(chunks, ("z", "l"), 0, 0, tiled=True, axis_index_groups=[down]).reshape(-1, 128)
    sent = reduce_chunks(got, 32, 32)
    second = [4 * a + l for a in SECOND for l in ((0, 1, 2, 3) if a > 3 else (3, 2, 1, 0))]
    every = lax.all_to_all(sent.reshape(32, 1, -1), ("h", "x", "l"), 0, 0, tiled=True, axis_index_groups=[second])
    terms = gram_part(every.reshape(-1, 128), 8, height, ("h", "x"))
    terms = pair_spread(lax.all_gather(terms, "c", axis=0, tiled=False), 8)
    parts = lax.all_to_all(terms, "z", 0, 0, tiled=True, axis_index_groups=[[6, 7, 5, 4, 2, 3, 1, 0]])
    gram, core = finish(parts, sent, rank * rank // 64, 1.0 / (rank * rank))
    return core, gram


def solution(mesh):
    fine = Mesh(mesh.devices.reshape(2, 4, 8, 2, 4), ("h", "x", "z", "c", "l"))
    placed = (P(("h", "x"), ("z", "c"), "l"), P(("z", "c"), None), P("l", None))
    return jax.shard_map(
        on_device,
        mesh=fine,
        in_specs=placed,
        out_specs=(P(("h", "x"), ("z", "c", "l")), P(("h", "x"), None)),
        check_vma=False,
    )
```

```python
import functools
import jax
import jax.numpy as jnp
from jax import lax
from jax.experimental import pallas as pl
from jax.experimental.pallas import tpu as pltpu
from jax.sharding import Mesh, PartitionSpec as P

F32, BF16 = jnp.float32, jnp.bfloat16
NT = (((1,), (1,)), ((), ()))
SECOND = (7, 6, 5, 4, 3, 2, 1, 0)


def halves(x):
    high = x.astype(BF16)
    return high, (x - high.astype(F32)).astype(BF16)


def rounded(x):
    high = x.astype(BF16).astype(F32)
    return high, x - high


def exact_nt(left, right):
    m = left.shape[0]
    lh, ll = halves(left)
    rh, rl = halves(right)
    both = lax.dot_general(jnp.concatenate([lh, ll], 0), rh, NT, preferred_element_type=F32)
    return both[:m] + both[m:] + lax.dot_general(lh, rl, NT, preferred_element_type=F32)


def project(slab_ref, two_ref, three_ref, keep_ref, send_ref, turned):
    step = pl.program_id(0)
    group, across, depth = slab_ref.shape
    rank = two_ref.shape[0]
    height = turned.shape[0] // rank
    first = exact_nt(three_ref[...], slab_ref[...].reshape(group * across, depth))
    for q in range(group):
        turned[pl.ds(step * group + q, rank, stride=height), :] = first[:, q * across : (q + 1) * across]

    @pl.when(step == pl.num_programs(0) - 1)
    def _():
        two = two_ref[...]
        turns = [two[r : r + 1] for c in range(2) for r in range(rank - 1, -1, -1) if r // 3 % 2 == c]
        done = exact_nt(jnp.concatenate(turns, 0), turned[...])
        half, tiles = rank // 2, rank * height // 128
        first_core = lax.axis_index("c") == 0
        keep = jnp.where(first_core, done[:half], done[half:])
        send = jnp.where(first_core, done[half:], done[:half])
        for t in range(tiles):
            keep_ref[pl.ds(tiles - 1 - t, half, stride=tiles), :] = keep[:, 128 * t : 128 * (t + 1)]
            send_ref[pl.ds(tiles - 1 - t, half, stride=tiles), :] = send[:, 128 * t : 128 * (t + 1)]


def front(slab, two, three, group=16):
    height, across, depth = slab.shape
    rank = two.shape[0]
    rows = rank * rank * height // 256
    return pl.pallas_call(
        project,
        grid=(height // group,),
        in_specs=[
            pl.BlockSpec((group, across, depth), lambda g: (g, 0, 0)),
            pl.BlockSpec((rank, across), lambda g: (0, 0)),
            pl.BlockSpec((rank, depth), lambda g: (0, 0)),
        ],
        out_specs=[pl.BlockSpec((rows, 128), lambda g: (0, 0))] * 2,
        out_shape=[pltpu.VMEM((rows, 128), F32)] * 2,
        scratch_shapes=[pltpu.VMEM((rank * height, across), F32)],
        compiler_params=pltpu.CompilerParams(vmem_limit_bytes=16 << 20),
        name="project",
    )(*(pltpu.with_memory_space_constraint(x, pltpu.HBM) for x in (slab, two, three)))


def gather_sum(n_parts, copies, got_ref, sent_ref, pattern):
    rows = got_ref.shape[0] // n_parts
    wide = 8 * rows
    total = got_ref[:wide, :]
    for b in range(1, n_parts // 8):
        total = total + got_ref[wide * b : wide * (b + 1), :]
    pattern[...] = total
    own = pattern[:rows, :]
    for b in range(1, 8):
        own = own + pattern[rows * b : rows * (b + 1), :]
    for b in range(8):
        pattern[rows * b : rows * (b + 1), :] = own
    total = pattern[...]
    for b in range(copies // 8):
        sent_ref[wide * b : wide * (b + 1), :] = total


def finish_all(scale, parts_ref, sent_ref, gram_ref, core_ref, cols):
    n_parts = parts_ref.shape[0]
    total = parts_ref[0]
    for b in range(1, n_parts):
        total = total + parts_ref[b]
    gram_ref[...] = total * scale
    height, n_cols = core_ref.shape
    per = 128 // height
    rows = n_cols // per
    own = sent_ref[:rows, :]
    for q in range(per):
        for m in range(rows):
            at = per * (rows - 1 - m) + q
            cols[at : at + 1, :] = own[m : m + 1, height * q : height * (q + 1)]
    core_ref[...] = cols[...].T


def finish(parts, sent, n_cols, scale):
    height, width = parts.shape[1:]
    return pl.pallas_call(
        functools.partial(finish_all, scale),
        out_shape=(jax.ShapeDtypeStruct((height, width), F32), jax.ShapeDtypeStruct((height, n_cols), F32)),
        scratch_shapes=[pltpu.VMEM((n_cols, height), F32)],
        compiler_params=pltpu.CompilerParams(vmem_limit_bytes=4 << 20),
        name="finish",
    )(*(pltpu.with_memory_space_constraint(x, pltpu.VMEM) for x in (parts, sent)))


def reduce_chunks(got, n_parts, copies):
    rows = got.shape[0] // n_parts
    return pl.pallas_call(
        functools.partial(gather_sum, n_parts, copies),
        out_shape=pltpu.VMEM((copies * rows, 128), F32),
        scratch_shapes=[pltpu.VMEM((8 * rows, 128), F32)],
        compiler_params=pltpu.CompilerParams(vmem_limit_bytes=4 << 20),
        name="reduce_chunks",
    )(pltpu.with_memory_space_constraint(got, pltpu.VMEM))


def gram_terms(n_rows, height, axes, all_ref, out_ref):
    me = lax.axis_index(axes)
    per = 128 // height
    deep = all_ref.shape[0] // n_rows
    at = [deep * SECOND.index(a) for a in range(n_rows)]
    blocks = [all_ref[s : s + deep, :] for s in at]
    piece = deep // 4
    for a in range(4, n_rows):
        blocks[a] = jnp.concatenate([blocks[a][piece * l : piece * (l + 1), :] for l in (3, 2, 1, 0)], 0)
    mine = jnp.zeros_like(blocks[0])
    for a in range(n_rows):
        mine = jnp.where(me == a, blocks[a], mine)
    lh, ll = rounded(mine)
    rh, rl = rounded(jnp.concatenate(blocks, 1))
    gap = jnp.zeros((-deep % 8, 128), F32)
    left = jnp.concatenate([lh, gap, ll, gap, lh, gap], 0).T.astype(BF16)
    gap = jnp.zeros((-deep % 8, rh.shape[1]), F32)
    right = jnp.concatenate([rh, gap, rh, gap, rl, gap], 0).astype(BF16)
    both = jnp.dot(left, right, preferred_element_type=F32)
    lane = lax.broadcasted_iota(jnp.int32, (height, 128), 1) // height
    folded = []
    for a in range(n_rows):
        z = both[:, 128 * a : 128 * (a + 1)]
        u = jnp.zeros((height, 128), F32)
        for q in range(per):
            u = jnp.where(lane == q, z[height * q : height * (q + 1), :], u)
        shift = 64
        while shift >= height:
            u = u + pltpu.roll(u, shift, 1)
            shift //= 2
        folded.append(u)
    for t in range(n_rows // per):
        u = folded[t * per]
        for q in range(1, per):
            u = jnp.where(lane == q, folded[t * per + q], u)
        out_ref[:, 128 * t : 128 * (t + 1)] = u


def gram_part(every, n_rows, height, axes):
    return pl.pallas_call(
        functools.partial(gram_terms, n_rows, height, axes),
        out_shape=pltpu.VMEM((height, n_rows * height), F32),
        compiler_params=pltpu.CompilerParams(vmem_limit_bytes=4 << 20),
        name="gram_part",
    )(pltpu.with_memory_space_constraint(every, pltpu.VMEM))


def add_other(axis, keep_ref, both_ref, out_ref):
    other = jnp.where(lax.axis_index(axis) == 0, both_ref[1], both_ref[0])
    out_ref[...] = keep_ref[...] + other


def core_sum(keep, both, axis):
    return pl.pallas_call(
        functools.partial(add_other, axis),
        out_shape=pltpu.VMEM(keep.shape, F32),
        compiler_params=pltpu.CompilerParams(vmem_limit_bytes=4 << 20),
        name="core_sum",
    )(*(pltpu.with_memory_space_constraint(x, pltpu.VMEM) for x in (keep, both)))


def spread_sum(pair_ref, out_ref):
    total = pair_ref[0] + pair_ref[1]
    for b in range(out_ref.shape[0]):
        out_ref[b] = total


def pair_spread(pair, copies):
    return pl.pallas_call(
        spread_sum,
        out_shape=pltpu.VMEM((copies,) + pair.shape[1:], F32),
        compiler_params=pltpu.CompilerParams(vmem_limit_bytes=4 << 20),
        name="pair_spread",
    )(pltpu.with_memory_space_constraint(pair, pltpu.VMEM))


def on_device(slab, factor_two, factor_three):
    height = slab.shape[0]
    rank = factor_two.shape[1]
    keep, send = front(slab, factor_two.T, factor_three.T)
    chunks = core_sum(keep, lax.all_gather(send, "c", axis=0, tiled=False), "c").reshape(32, 1, -1)
    down = list(range(31, -1, -1))
    got = lax.all_to_all(chunks, ("z", "l"), 0, 0, tiled=True, axis_index_groups=[down]).reshape(-1, 128)
    sent = reduce_chunks(got, 32, 32)
    second = [4 * a + l for a in SECOND for l in ((0, 1, 2, 3) if a > 3 else (3, 2, 1, 0))]
    every = lax.all_to_all(sent.reshape(32, 1, -1), ("h", "x", "l"), 0, 0, tiled=True, axis_index_groups=[second])
    terms = gram_part(every.reshape(-1, 128), 8, height, ("h", "x"))
    terms = pair_spread(lax.all_gather(terms, "c", axis=0, tiled=False), 8)
    parts = lax.all_to_all(terms, "z", 0, 0, tiled=True, axis_index_groups=[[6, 7, 5, 4, 2, 3, 1, 0]])
    gram, core = finish(parts, sent, rank * rank // 64, 1.0 / (rank * rank))
    return core, gram


def solution(mesh):
    fine = Mesh(mesh.devices.reshape(2, 4, 8, 2, 4), ("h", "x", "z", "c", "l"))
    placed = (P(("h", "x"), ("z", "c"), "l"), P(("z", "c"), None), P("l", None))
    return jax.shard_map(
        on_device,
        mesh=fine,
        in_specs=placed,
        out_specs=(P(("h", "x"), ("z", "c", "l")), P(("h", "x"), None)),
        check_vma=False,
    )
```
